256 devices in a mesh: dp: 256 (over y, z, x, core).
Axes of the slice: x: 4, y: 4, z: 8, core: 2. Of those that a mesh axis runs over, the one named last changes fastest.
Arguments:
- train_features: bfloat16 [262144, 1024], P('dp'), as said below
- target_features: bfloat16 [32768, 1024], P('dp'), may hold values from -6 to 6
Outputs:
- scores: float32 [262144, 512], P('dp')
The draws below stay inside these ranges and needn't reach their ends.
Inputs may be any that keep to these rules, and one draw needn't show every extreme that they name: `train_features`: Real-valued features of varied scales per example and per feature, correlated between neighbouring features.
All inputs are finite; a program needn't handle non-finite values.
Results may differ from the reference program's by a relative error of at most 0.00035.
Values may be sent and summed in bfloat16 or wider, within the bound.
No kernel may reach another device: no remote copies, remote signals or barrier semaphores. Data moves between devices by JAX's collectives and lax.ppermute only.
A program may use at most 128 MiB of HBM per device.

```python
import math
import jax
import jax.numpy as jnp
from jax import lax

K = 1024
TRAIN_DEV = 1024
TGT_DEV = 128
STEPS = 4
NTRAIN = 262144
TARGETS = 32768
N_DP = 256


def draw_train_features(key, part):
    key = jax.random.fold_in(key, 1)
    keys = jax.random.split(key, 5)
    noise = jax.random.normal(keys[0], (NTRAIN, K), jnp.float32)
    common_weight = 0.5
    rolled = jnp.roll(noise, 1, axis=1)
    column_scale = jnp.exp(jax.random.uniform(keys[1], (1, K), jnp.float32, math.log(0.5), math.log(2.0)))
    position = jnp.arange(NTRAIN, dtype=jnp.float32).reshape(NTRAIN, 1)
    row_scale = jnp.exp(jax.random.uniform(keys[2], (NTRAIN, 1), jnp.float32, 0.0, math.log(10.0)))
    row_scale = row_scale * jnp.sqrt(1.0 + 2.0 * position / NTRAIN)
    shared_rows = jax.random.normal(keys[3], (NTRAIN, 1), jnp.float32)
    shared_cols = jax.random.normal(keys[4], (1, K), jnp.float32)
    values = row_scale * (column_scale * (noise + 0.8 * rolled) + common_weight * shared_rows * shared_cols)
    return values.astype(jnp.bfloat16)


def block_scale(own_key, dims, cuts, low, high):
    loudness, own = 1.0, jax.random.fold_in(own_key, 6)
    for axis_at, blocks in cuts:
        heights = jnp.exp(jax.random.uniform(jax.random.fold_in(own, axis_at), (blocks,), jnp.float32, low / len(cuts), high / len(cuts)))
        loudness = loudness * jnp.repeat(heights, dims[axis_at] // blocks).reshape([-1 if axis == axis_at else 1 for axis in range(len(dims))])
    return loudness


def normal_values(own_key, extent, width, most, cuts=(), held_as=jnp.bfloat16):
    factor_of = block_scale(own_key, extent, cuts, -0.22, 0.18) if cuts else 1.0
    values = jax.random.normal(own_key, extent, jnp.float32) * width * factor_of
    return jnp.minimum(jnp.maximum(values, -most), most).astype(held_as)


def setup_inputs(seed: int = 0) -> dict:
    streams_of = jax.random.split(jax.random.key(seed), 3)
    train_features = draw_train_features(jax.random.fold_in(streams_of[2], 71), 0)
    target_features = normal_values(streams_of[1], (TARGETS, K), 1.0, 6.0, ((0, 256),))
    return dict(train_features=train_features, target_features=target_features)


def solve_right(factor, row_block):
    inner = lax.linalg.triangular_solve(factor, row_block, left_side=False, lower=True, transpose_a=True)
    return lax.linalg.triangular_solve(factor, inner, left_side=False, lower=True, transpose_a=False)

def reference(train_features, target_features):
    gram_sum = jnp.dot(train_features.T.astype(jnp.float32), train_features.astype(jnp.float32), preferred_element_type=jnp.float32)
    damping = 0.1 * jnp.trace(gram_sum) / K
    damped = gram_sum + damping * jnp.eye(K, dtype=jnp.float32)
    factor = jnp.linalg.cholesky(damped)
    solved = solve_right(factor, target_features.astype(jnp.float32))
    grouped = train_features.reshape(N_DP, TRAIN_DEV, K)

    def score_device(packed):
        device, row_block = packed
        pieces = []
        for offset in range(STEPS):
            start = ((device - offset) % N_DP * TGT_DEV).astype(jnp.int32)
            pieces.append(lax.dynamic_slice_in_dim(solved, start, TGT_DEV, 0))
        stacked = jnp.concatenate(pieces, axis=0)
        return lax.dot_general(row_block.astype(jnp.float32), stacked, (((1,), (1,)), ((), ())), precision=lax.Precision.HIGHEST)
    result = lax.map(score_device, (jnp.arange(N_DP, dtype=jnp.int32), grouped))
    result = result.reshape(NTRAIN, STEPS * TGT_DEV)
    return result * math.sqrt(NTRAIN / K)
```

```python
import functools
import math

import jax
import jax.numpy as jnp
from jax import lax
from jax.experimental import pallas as pl
from jax.experimental.pallas import tpu as pltpu
from jax.sharding import PartitionSpec as P

STEPS = 4
LEAF = 128
GROUP = 8
GRID = (4, 8, 4, 2)
Y, Z, X, CORE = range(4)
F32 = jnp.float32
BF16 = jnp.bfloat16
VMEM = pl.BlockSpec(memory_space=pltpu.VMEM)
SMEM = pl.BlockSpec(memory_space=pltpu.SMEM)
ROOM = pltpu.CompilerParams(vmem_limit_bytes=56 * 1024 * 1024)


def place(device):
    where = []
    for size in reversed(GRID):
        where.append(device % size)
        device //= size
    return where[::-1]


def device_at(where):
    device = 0
    for size, at in zip(GRID, where):
        device = device * size + at
    return device


def along(axis, move):
    route = []
    for device in range(math.prod(GRID)):
        where = place(device)
        where[axis] = move(where[axis]) % GRID[axis]
        route.append((device, device_at(where)))
    return route


def shifted(block, axis, distance):
    return lax.ppermute(block, "dp", along(axis, lambda p: p + distance))


def swapped(block, axis, mask):
    return lax.ppermute(block, "dp", along(axis, lambda p: p ^ mask))


def passed_along(block, distance):
    devices = math.prod(GRID)
    return lax.ppermute(block, "dp", [((i - distance) % devices, i) for i in range(devices)])


def mm(left, right, dims=((1,), (0,))):
    return lax.dot_general(left, right, (dims, ((), ())), preferred_element_type=F32)


def mm_wide(left, right):
    return lax.dot_general(
        left, right, (((1,), (0,)), ((), ())), precision=lax.Precision.HIGHEST, preferred_element_type=F32
    )


def split(value):
    high = value.astype(BF16)
    return high, (value - high.astype(F32)).astype(BF16)


def mm_split(left, right, dims=((1,), (0,))):
    return mm(left[0], right[0], dims) + (mm(left[0], right[1], dims) + mm(left[1], right[0], dims))


def blocks_of(width):
    count = width // LEAF
    return [(i, j) for i in range(count) for j in range(i, count)]


def gram_kernel(which_ref, x_ref, out_ref):
    pairs = blocks_of(x_ref.shape[1])
    half = len(pairs) // 2
    for part in range(2):

        @pl.when(which_ref[0] == part)
        def _():
            mine = pairs[part * half : (part + 1) * half]
            for i in sorted({pair[0] for pair in mine}):
                columns = [j for row, j in mine if row == i]
                lo, hi = columns[0] * LEAF, (columns[-1] + 1) * LEAF
                product = mm(x_ref[:, i * LEAF : (i + 1) * LEAF], x_ref[:, lo:hi], ((0,), (0,)))
                at = mine.index((i, columns[0])) * LEAF
                for n in range(len(columns)):
                    out_ref[at + n * LEAF : at + (n + 1) * LEAF, :] = product[:, n * LEAF : (n + 1) * LEAF]


def gram_half(features, which):
    rows = len(blocks_of(features.shape[1])) // 2 * LEAF
    return pl.pallas_call(
        gram_kernel,
        out_shape=jax.ShapeDtypeStruct((rows, LEAF), F32),
        in_specs=[SMEM, VMEM],
        out_specs=VMEM,
        compiler_params=ROOM,
        name="gram_half",
    )(which, features)


def sum_and_cut_kernel(terms, at_ref, *refs):
    sources, pieces = refs[:terms], refs[terms:]
    rows = pieces[0].shape[0]
    for d, piece in enumerate(pieces):
        start = pl.multiple_of(lax.rem(at_ref[0] + d, len(pieces)) * rows, 8)
        total = sources[0][pl.ds(start, rows), :]
        for source in sources[1:]:
            total = total + source[pl.ds(start, rows), :]
        piece[...] = total


def sum_and_cut(sources, at, pieces):
    rows, width = sources[0].shape
    return pl.pallas_call(
        functools.partial(sum_and_cut_kernel, len(sources)),
        out_shape=[jax.ShapeDtypeStruct((rows // pieces, width), F32)] * pieces,
        in_specs=[SMEM] + [VMEM] * len(sources),
        out_specs=[VMEM] * pieces,
        compiler_params=ROOM,
        name="sum_and_cut",
    )(at, *sources)


def lay_out_kernel(at_ref, *refs):
    pieces, out_ref = refs[:-1], refs[-1]
    rows = pieces[0].shape[0]
    for d, piece in enumerate(pieces):
        start = pl.multiple_of(lax.rem(at_ref[0] + len(pieces) - d, len(pieces)) * rows, 8)
        out_ref[pl.ds(start, rows), :] = piece[...]


def lay_out(pieces, at):
    rows, width = pieces[0].shape
    return pl.pallas_call(
        lay_out_kernel,
        out_shape=jax.ShapeDtypeStruct((rows * len(pieces), width), F32),
        in_specs=[SMEM] + [VMEM] * len(pieces),
        out_specs=VMEM,
        compiler_params=ROOM,
        name="lay_out",
    )(at, *pieces)


def invert(rows):
    rows = list(rows)
    count, shape = len(rows), rows[0].shape
    lane = lax.broadcasted_iota(jnp.int32, shape, 1)
    sub = lax.broadcasted_iota(jnp.int32, shape, 0)

    def column(value, at):
        return jnp.broadcast_to(value[:, at : at + 1], shape)

    def row(value, at):
        return jnp.broadcast_to(value[at : at + 1, :], shape)

    for g in range(count):
        first = GROUP * g
        inside = (lane >= first) & (lane < first + GROUP)
        columns = [column(rows[g], first + q) for q in range(GROUP)]
        wide = jnp.where(inside, jnp.where(lane - first == sub, 1.0, 0.0), rows[g])
        for p in range(0, GROUP, 2):
            u, v = columns[p], columns[p + 1]
            a, b, c, d = row(u, p), row(v, p), row(u, p + 1), row(v, p + 1)
            scale = 1.0 / (a * d - b * c)

            def eliminated(value):
                r0, r1 = row(value, p), row(value, p + 1)
                n0 = (d * r0 - b * r1) * scale
                n1 = (a * r1 - c * r0) * scale
                return jnp.where(sub == p, n0, jnp.where(sub == p + 1, n1, value - u * n0 - v * n1))

            for q in range(p + 2, GROUP):
                columns[q] = eliminated(columns[q])
            wide = eliminated(wide)
        pivot_rows = [row(wide, q) for q in range(GROUP)]
        for i in [(g + 1 + n) % count for n in range(count - 1)]:
            terms = [column(rows[i], first + q) * pivot_rows[q] for q in range(GROUP)]
            while len(terms) > 1:
                terms = [terms[n] + terms[n + 1] for n in range(0, len(terms), 2)]
            rows[i] = jnp.where(inside, 0.0, rows[i]) - terms[0]
        rows[g] = wide
    return rows


def attribution_kernel(scale, pieces, where_ref, *refs):
    piece_refs, target_refs = refs[:pieces], refs[pieces : pieces + STEPS]
    x_ref, out_ref, packed_ref, a_ref, t_ref, w_ref = refs[pieces + STEPS :]
    width = a_ref.shape[0]
    steps = width // LEAF
    rows = piece_refs[0].shape[0]
    for n, piece in enumerate(piece_refs):
        packed_ref[pl.ds(pl.multiple_of(where_ref[n] * rows, 8), rows), :] = piece[...]
    for n, (i, j) in enumerate(blocks_of(width)):
        a_ref[i * LEAF : (i + 1) * LEAF, j * LEAF : (j + 1) * LEAF] = packed_ref[n * LEAF : (n + 1) * LEAF, :]
    tile = (LEAF, LEAF)
    diagonal = lax.broadcasted_iota(jnp.int32, tile, 0) == lax.broadcasted_iota(jnp.int32, tile, 1)
    total = jnp.zeros(tile, F32)
    for j in range(steps):
        s = slice(j * LEAF, (j + 1) * LEAF)
        total = total + jnp.where(diagonal, a_ref[s, s], 0.0)
    damping = 0.1 * jnp.sum(total, keepdims=True) / width
    for j in range(steps):
        s = slice(j * LEAF, (j + 1) * LEAF)
        a_ref[s, s] = a_ref[s, s] + jnp.where(diagonal, damping, 0.0)
    for j, target in enumerate(target_refs):
        t_ref[j * target.shape[0] : (j + 1) * target.shape[0], :] = target[...].astype(F32)
    for j in range(steps):
        lo, hi = j * LEAF, (j + 1) * LEAF
        groups = [a_ref[lo + GROUP * i : lo + GROUP * (i + 1), lo:hi] for i in range(LEAF // GROUP)]
        inverse = jnp.concatenate(invert(groups), axis=0)
        tj = split(t_ref[:, lo:hi])
        if hi < width:
            u = a_ref[lo:hi, hi:]
            w = mm_wide(inverse, u)
            w_ref[lo:hi, hi:] = w
            u, w = split(u), split(w)
            for r in range(hi, width, LEAF):
                left = tuple(part[:, r - hi : r - hi + LEAF] for part in u)
                right = tuple(part[:, r - hi :] for part in w)
                a_ref[r : r + LEAF, r:] = a_ref[r : r + LEAF, r:] - mm_split(left, right, ((0,), (0,)))
            t_ref[:, hi:] = t_ref[:, hi:] - mm_split(tj, w)
        t_ref[:, lo:hi] = mm_split(tj, split(inverse))
    for j in range(steps - 2, -1, -1):
        lo, hi = j * LEAF, (j + 1) * LEAF
        known, w = split(t_ref[:, hi:]), split(w_ref[lo:hi, hi:])
        t_ref[:, lo:hi] = t_ref[:, lo:hi] - mm_split(known, w, ((1,), (1,)))
    solved = split(t_ref[...])
    x = x_ref[...]
    out_ref[...] = (mm(x, solved[0], ((1,), (1,))) + mm(x, solved[1], ((1,), (1,)))) * scale


def attribute(pieces, where, targets, x, scale):
    width = x.shape[1]
    asked = STEPS * targets[0].shape[0]
    packed = sum(piece.shape[0] for piece in pieces)
    return pl.pallas_call(
        functools.partial(attribution_kernel, scale, len(pieces)),
        out_shape=jax.ShapeDtypeStruct((x.shape[0], asked), F32),
        in_specs=[SMEM] + [VMEM] * (len(pieces) + STEPS + 1),
        out_specs=VMEM,
        scratch_shapes=[
            pltpu.VMEM((packed, LEAF), F32),
            pltpu.VMEM((width, width), F32),
            pltpu.VMEM((asked, width), F32),
            pltpu.VMEM((width, width), F32),
        ],
        compiler_params=ROOM,
        name="attribute",
    )(where, *pieces, *targets, x)


def local(train_features, target_features):
    width = train_features.shape[1]
    examples = train_features.shape[0] * math.prod(GRID)
    device = lax.axis_index("dp")
    core = device % GRID[CORE]
    x_at = device // GRID[CORE] % GRID[X]
    y_at = device // math.prod(GRID[Z:])
    nx, ny = GRID[X], GRID[Y]

    sent = gram_half(train_features, (1 - core).reshape(1))
    taken = swapped(sent, CORE, 1)
    kept = gram_half(train_features, core.reshape(1))

    cut = sum_and_cut([kept, taken], x_at.reshape(1), nx)
    cut = [cut[0]] + [shifted(cut[d], X, d) for d in range(1, nx)]
    cut = sum_and_cut(cut, y_at.reshape(1), ny)
    cut = [cut[0]] + [shifted(cut[d], Y, d) for d in range(1, ny)]
    share = (cut[0] + cut[1]) + (cut[2] + cut[3])

    share, own_targets = lax.optimization_barrier((share, target_features))
    targets = [own_targets] + [passed_along(own_targets, d) for d in range(1, STEPS)]
    for mask in (1, 3, 7):
        share = share + swapped(share, Z, mask)

    parts = [share] + [shifted(share, Y, d) for d in range(1, ny)]
    part = lay_out(parts, y_at.reshape(1))
    part, targets = lax.optimization_barrier((part, targets))
    halves = [part] + [shifted(part, X, d) for d in range(1, nx)]
    numbers = [core * nx + (x_at - d) % nx for d in range(nx)]
    halves += [swapped(half, CORE, 1) for half in halves]
    numbers += [(1 - core) * nx + (x_at - d) % nx for d in range(nx)]
    return attribute(
        halves, jnp.stack(numbers).astype(jnp.int32), targets, train_features, math.sqrt(examples / width)
    )


def solution(mesh):
    placed = (P("dp", None), P("dp", None))
    return jax.shard_map(local, mesh=mesh, in_specs=placed, out_specs=P("dp", None), check_vma=False)
```

```python
import functools
import math

import jax
import jax.numpy as jnp
from jax import lax
from jax.experimental import pallas as pl
from jax.experimental.pallas import tpu as pltpu
from jax.sharding import PartitionSpec as P

STEPS = 4
LEAF = 128
GROUP = 8
BAND = 64
GRID = (4, 8, 4, 2)
Y, Z, X, CORE = range(4)
F32 = jnp.float32
BF16 = jnp.bfloat16
VMEM = pl.BlockSpec(memory_space=pltpu.VMEM)
SMEM = pl.BlockSpec(memory_space=pltpu.SMEM)
ROOM = pltpu.CompilerParams(vmem_limit_bytes=56 * 1024 * 1024)


def place(device):
    where = []
    for size in reversed(GRID):
        where.append(device % size)
        device //= size
    return where[::-1]


def device_at(where):
    device = 0
    for size, at in zip(GRID, where):
        device = device * size + at
    return device


def along(axis, move):
    route = []
    for device in range(math.prod(GRID)):
        where = place(device)
        where[axis] = move(where[axis]) % GRID[axis]
        route.append((device, device_at(where)))
    return route


def shifted(block, axis, distance):
    return lax.ppermute(block, "dp", along(axis, lambda p: p + distance))


def swapped(block, axis, mask):
    return lax.ppermute(block, "dp", along(axis, lambda p: p ^ mask))


def passed_along(block, distance):
    devices = math.prod(GRID)
    return lax.ppermute(block, "dp", [((i - distance) % devices, i) for i in range(devices)])


def mm(left, right, dims=((1,), (0,))):
    return lax.dot_general(left, right, (dims, ((), ())), preferred_element_type=F32)


def mm_wide(left, right):
    return lax.dot_general(
        left, right, (((1,), (0,)), ((), ())), precision=lax.Precision.HIGHEST, preferred_element_type=F32
    )


def split(value):
    high = value.astype(BF16)
    return high, (value - high.astype(F32)).astype(BF16)


def mm_split(left, right, dims=((1,), (0,))):
    return mm(left[0], right[0], dims) + (mm(left[0], right[1], dims) + mm(left[1], right[0], dims))


def blocks_of(width):
    count = width // LEAF
    return [(i, j) for i in range(count) for j in range(i, count)]


def gram_kernel(which_ref, x_ref, out_ref):
    pairs = blocks_of(x_ref.shape[1])
    half = len(pairs) // 2
    for part in range(2):

        @pl.when(which_ref[0] == part)
        def _():
            mine = pairs[part * half : (part + 1) * half]
            for i in sorted({pair[0] // 2 * 2 for pair in mine}):
                inside = [pair for pair in mine if pair[0] in (i, i + 1)]
                top, bottom = inside[0][0], inside[-1][0] + 1
                left, right = min(j for _, j in inside), max(j for _, j in inside) + 1
                rows, columns = slice(top * LEAF, bottom * LEAF), slice(left * LEAF, right * LEAF)
                product = mm(x_ref[:, rows], x_ref[:, columns], ((0,), (0,)))
                for row, j in inside:
                    at = mine.index((row, j)) * LEAF
                    down, over = (row - top) * LEAF, (j - left) * LEAF
                    out_ref[at : at + LEAF, :] = product[down : down + LEAF, over : over + LEAF]


def gram_half(features, which):
    rows = len(blocks_of(features.shape[1])) // 2 * LEAF
    return pl.pallas_call(
        gram_kernel,
        out_shape=jax.ShapeDtypeStruct((rows, LEAF), F32),
        in_specs=[SMEM, VMEM],
        out_specs=VMEM,
        compiler_params=ROOM,
        name="gram_half",
    )(which, features)


def cut_along(sources, first, rows, axis, at):
    count = GRID[axis]
    rows = rows // count

    def piece(d):
        start = first + (at + d) % count * rows
        return sum(lax.dynamic_slice_in_dim(source, start, rows, 0) for source in sources)

    return [shifted(piece(d), axis, d) for d in range(1, count)] + [piece(0)]


def gathered_along(piece, axis):
    return [piece] + [shifted(piece, axis, d) for d in range(1, GRID[axis])]


def onward(pieces):
    return jnp.concatenate([pieces[0]] + pieces[:0:-1], axis=0)


def summed(kept, taken, core, at, target_features):
    rows = kept.shape[0] // 2
    orders = ((Y, X), (X, Y))
    first = [cut_along([kept, taken], n * rows, rows, order[0], at[order[0]]) for n, order in enumerate(orders)]
    second = []
    for order, sources in zip(orders, first):
        second.append(cut_along(sources, 0, rows // GRID[order[0]], order[1], at[order[1]]))
    share = jnp.concatenate([sum(sources) for sources in second], axis=0)
    share, late = lax.optimization_barrier((share, target_features))
    late = passed_along(late, STEPS - 1)
    for mask in (1, 3, 7):
        share = share + swapped(share, Z, mask)
    share, late = lax.optimization_barrier((share, late))
    least = share.shape[0] // 2
    pieces, numbers = [], []
    for n, order in enumerate(orders):
        near, far = order[1], order[0]
        part = onward(gathered_along(share[n * least : (n + 1) * least], near))
        for d, piece in enumerate(gathered_along(part, far)):
            pieces.append(piece)
            numbers += [
                (n * GRID[far] + (at[far] - d) % GRID[far]) * GRID[near] + (at[near] + r) % GRID[near]
                for r in range(GRID[near])
            ]
    numbers = jnp.stack(numbers).astype(jnp.int32)
    half = kept.shape[0] // least
    pieces += [swapped(piece, CORE, 1) for piece in pieces]
    return pieces, jnp.concatenate([numbers + core * half, numbers + (1 - core) * half]), late


def invert(rows, meanwhile):
    rows = list(rows)
    count, shape = len(rows), rows[0].shape
    per_band = BAND // GROUP
    lane = lax.broadcasted_iota(jnp.int32, shape, 1)
    sub = lax.broadcasted_iota(jnp.int32, shape, 0)

    def column(value, at):
        return jnp.take_along_axis(value, jnp.full(shape, at, jnp.int32), axis=1)

    def row(value, at):
        return jnp.broadcast_to(value[at : at + 1, :], shape)

    for g in range(count):
        first = GROUP * g
        band = range(g // per_band * per_band, (g // per_band + 1) * per_band)
        inside = (lane >= first) & (lane < first + GROUP)
        columns = [column(rows[g], first + q) for q in range(GROUP)]
        wide = jnp.where(inside, jnp.where(lane - first == sub, 1.0, 0.0), rows[g])
        for p in range(0, GROUP, 2):
            u, v = columns[p], columns[p + 1]
            a, b, c, d = row(u, p), row(v, p), row(u, p + 1), row(v, p + 1)
            scale = 1.0 / (a * d - b * c)

            def eliminated(value):
                r0, r1 = row(value, p), row(value, p + 1)
                n0 = (d * r0 - b * r1) * scale
                n1 = (a * r1 - c * r0) * scale
                return jnp.where(sub == p, n0, jnp.where(sub == p + 1, n1, value - u * n0 - v * n1))

            for q in range(p + 2, GROUP):
                columns[q] = eliminated(columns[q])
            wide = eliminated(wide)
        pivot_rows = [row(wide, q) for q in range(GROUP)]
        for i in [band[(g + 1 + n) % per_band] for n in range(per_band - 1)]:
            terms = [column(rows[i], first + q) * pivot_rows[q] for q in range(GROUP)]
            while len(terms) > 1:
                terms = [terms[n] + terms[n + 1] for n in range(0, len(terms), 2)]
            rows[i] = jnp.where(inside, 0.0, rows[i]) - terms[0]
        rows[g] = wide
        meanwhile(g)
        if g == band[-1]:
            swept = (lane >= GROUP * band[0]) & (lane < GROUP * (band[-1] + 1))
            others = [i for i in range(count) if i not in band]
            left = jnp.concatenate([jnp.where(swept, rows[i], 0.0) for i in others], axis=0)
            right = jnp.concatenate([rows[i] if i in band else jnp.zeros(shape, F32) for i in range(count)], axis=0)
            product = mm_wide(left, right)
            for n, i in enumerate(others):
                rows[i] = jnp.where(swept, 0.0, rows[i]) - product[n * GROUP : (n + 1) * GROUP]
    return rows


def attribution_kernel(scale, pieces, where_ref, *refs):
    piece_refs, target_refs = refs[:pieces], refs[pieces : pieces + STEPS]
    x_ref, out_ref, packed_ref, m_ref, left_ref, right_ref, solved_ref = refs[pieces + STEPS :]
    examples, width = x_ref.shape
    asked = out_ref.shape[1]
    steps = width // LEAF
    slots = LEAF // GROUP
    cuts = where_ref.shape[0] // pieces
    rows = piece_refs[0].shape[0] // cuts
    for n in range(pieces * cuts):
        piece, first = piece_refs[n // cuts], n % cuts * rows
        packed_ref[pl.ds(pl.multiple_of(where_ref[n] * rows, 8), rows), :] = piece[first : first + rows, :]
    tile = (LEAF, LEAF)
    diagonal = lax.broadcasted_iota(jnp.int32, tile, 0) == lax.broadcasted_iota(jnp.int32, tile, 1)
    blocks = {pair: slice(n * LEAF, (n + 1) * LEAF) for n, pair in enumerate(blocks_of(width))}
    total = jnp.zeros(tile, F32)
    for j in range(steps):
        total = total + jnp.where(diagonal, packed_ref[blocks[j, j], :], 0.0)
    damping = 0.1 * jnp.sum(total, keepdims=True) / width

    targets_at, examples_at, m_rows = width, width + asked, width + asked + examples

    def unpack(i, j):
        block = packed_ref[blocks[i, j], :]
        if i == j:
            m_ref[i * LEAF : (i + 1) * LEAF, j * LEAF : (j + 1) * LEAF] = block + jnp.where(diagonal, damping, 0.0)
        else:
            m_ref[i * LEAF : (i + 1) * LEAF, j * LEAF : (j + 1) * LEAF] = block
            m_ref[j * LEAF : (j + 1) * LEAF, i * LEAF : (i + 1) * LEAF] = block.T

    def widen(source, first, at, count):
        m_ref[at : at + count, :] = source[first : first + count, :].astype(F32)

    def both(ref, at, value, down):
        high, low = split(value)
        for n, part in enumerate((high, low, high) if down else (high, high, low)):
            if down:
                ref[n * LEAF : (n + 1) * LEAF, at : at + value.shape[1]] = part
            else:
                ref[at : at + value.shape[0], n * LEAF : (n + 1) * LEAF] = part

    def product_columns(inverse, lo, first, last):
        both(right_ref, first, mm_wide(inverse, m_ref[lo : lo + LEAF, first:last]), True)

    def split_rows(lo, first, last):
        both(left_ref, first, m_ref[first:last, lo : lo + LEAF], False)

    def update(r0, r1, c0, c1):
        m_ref[r0:r1, c0:c1] = m_ref[r0:r1, c0:c1] - mm(left_ref[r0:r1, :], right_ref[:, c0:c1])

    def weigh_targets(inverse, lo):
        high, low = split(mm_split(split(m_ref[targets_at:examples_at, lo : lo + LEAF]), split(inverse * scale)))
        for n, part in enumerate((high, low, high)):
            solved_ref[:, n * LEAF : (n + 1) * LEAF] = part

    def score(j, first, last):
        part = mm(left_ref[examples_at + first : examples_at + last, :], solved_ref[...], ((1,), (1,)))
        out_ref[first:last, :] = part if j == 0 else out_ref[first:last, :] + part

    def jobs_after(j, inverse):
        lo, hi = j * LEAF, (j + 1) * LEAF
        tall = [(r, min(r + 512, width)) for r in range(hi, width, 512)]
        tall += [(r, r + 512) for r in range(targets_at, m_rows, 512)]
        jobs = []
        if hi + LEAF < width:
            jobs.append(lambda: product_columns(inverse, lo, hi + LEAF, width))
        jobs.append(lambda: weigh_targets(inverse, lo))
        for r0, r1 in tall:
            fresh = max(r0, hi + LEAF) if r0 < targets_at else r0
            if fresh < r1:
                jobs.append(functools.partial(split_rows, lo, fresh, r1))
            if r0 >= targets_at:
                for c in range(hi, width, 256):
                    jobs.append(functools.partial(update, r0, r1, c, min(c + 256, width)))
                continue
            if fresh < r1:
                jobs.append(functools.partial(update, fresh, r1, hi, hi + LEAF))
            for c in range(hi + LEAF, width, 256):
                jobs.append(functools.partial(update, r0, r1, c, min(c + 256, width)))
        for r in range(0, examples, 256):
            jobs.append(functools.partial(score, j, r, r + 256))
        return jobs

    unpack(0, 0)
    jobs = [functools.partial(unpack, i, j) for i, j in blocks if (i, j) != (0, 0)]
    for j, target in enumerate(target_refs):
        jobs.append(functools.partial(widen, target, 0, targets_at + j * target.shape[0], target.shape[0]))
    for r in range(0, examples, 256):
        jobs.append(functools.partial(widen, x_ref, r, examples_at + r, 256))
    for j in range(steps):
        lo, hi = j * LEAF, (j + 1) * LEAF

        def meanwhile(g):
            for job in jobs[g * len(jobs) // slots : (g + 1) * len(jobs) // slots]:
                job()

        groups = [m_ref[lo + GROUP * i : lo + GROUP * (i + 1), lo:hi] for i in range(slots)]
        inverse = jnp.concatenate(invert(groups, meanwhile), axis=0)
        if hi < width:
            product_columns(inverse, lo, hi, hi + LEAF)
            split_rows(lo, hi, hi + LEAF)
            update(hi, hi + LEAF, hi, hi + LEAF)
            jobs = jobs_after(j, inverse)
    weigh_targets(inverse, lo)
    split_rows(lo, examples_at, m_rows)
    for r in range(0, examples, 256):
        score(steps - 1, r, r + 256)


def attribute(pieces, where, targets, x, scale):
    width = x.shape[1]
    asked = STEPS * targets[0].shape[0]
    packed = sum(piece.shape[0] for piece in pieces)
    return pl.pallas_call(
        functools.partial(attribution_kernel, scale, len(pieces)),
        out_shape=jax.ShapeDtypeStruct((x.shape[0], asked), F32),
        in_specs=[SMEM] + [VMEM] * (len(pieces) + STEPS + 1),
        out_specs=VMEM,
        scratch_shapes=[
            pltpu.VMEM((packed, LEAF), F32),
            pltpu.VMEM((width + asked + x.shape[0], width), F32),
            pltpu.VMEM((width + asked + x.shape[0], 3 * LEAF), BF16),
            pltpu.VMEM((3 * LEAF, width), BF16),
            pltpu.VMEM((asked, 3 * LEAF), BF16),
        ],
        compiler_params=ROOM,
        name="attribute",
    )(where, *pieces, *targets, x)


def local(train_features, target_features):
    width = train_features.shape[1]
    examples = train_features.shape[0] * math.prod(GRID)
    device = lax.axis_index("dp")
    core = device % GRID[CORE]
    at = {X: device // GRID[CORE] % GRID[X], Y: device // math.prod(GRID[Z:])}
    early = [passed_along(target_features, d) for d in range(1, STEPS - 1)]
    sent = gram_half(train_features, (1 - core).reshape(1))
    taken = swapped(sent, CORE, 1)
    kept = gram_half(train_features, core.reshape(1))
    kept, taken, early = lax.optimization_barrier((kept, taken, early))
    pieces, where, late = summed(kept, taken, core, at, target_features)
    targets = [target_features] + early + [late]
    return attribute(pieces, where, targets, train_features, math.sqrt(examples / width))


def solution(mesh):
    placed = (P("dp", None), P("dp", None))
    return jax.shard_map(local, mesh=mesh, in_specs=placed, out_specs=P("dp", None), check_vma=False)
```

```python
import functools
import math

import jax
import jax.numpy as jnp
from jax import lax
from jax.experimental import pallas as pl
from jax.experimental.pallas import tpu as pltpu
from jax.sharding import PartitionSpec as P

STEPS = 4
LEAF = 128
GROUP = 8
BAND = 64
GRID = (4, 8, 4, 2)
Y, Z, X, CORE = range(4)
F32 = jnp.float32
BF16 = jnp.bfloat16
VMEM = pl.BlockSpec(memory_space=pltpu.VMEM)
ANY = pl.BlockSpec(memory_space=pl.ANY)
SMEM = pl.BlockSpec(memory_space=pltpu.SMEM)
ROOM = pltpu.CompilerParams(vmem_limit_bytes=56 * 1024 * 1024)


def place(device):
    where = []
    for size in reversed(GRID):
        where.append(device % size)
        device //= size
    return where[::-1]


def device_at(where):
    device = 0
    for size, at in zip(GRID, where):
        device = device * size + at
    return device


def along(axis, move):
    route = []
    for device in range(math.prod(GRID)):
        where = place(device)
        where[axis] = move(where[axis]) % GRID[axis]
        route.append((device, device_at(where)))
    return route


def shifted(block, axis, distance):
    return lax.ppermute(block, "dp", along(axis, lambda p: p + distance))


def swapped(block, axis, mask):
    return lax.ppermute(block, "dp", along(axis, lambda p: p ^ mask))


def passed_along(block, distance):
    devices = math.prod(GRID)
    return lax.ppermute(block, "dp", [((i - distance) % devices, i) for i in range(devices)])


def mm(left, right, dims=((1,), (0,))):
    return lax.dot_general(left, right, (dims, ((), ())), preferred_element_type=F32)


def split_wide(value):
    high = value.astype(BF16)
    rest = value - high.astype(F32)
    middle = rest.astype(BF16)
    return high, middle, (rest - middle.astype(F32)).astype(BF16)


def mm_wide(left, right):
    high, middle, low = split_wide(left)
    above, between, below = split_wide(right)
    return mm(
        jnp.concatenate([high, high, high, middle, middle, low], axis=1),
        jnp.concatenate([above, between, below, above, between, above], axis=0),
    )


def split(value):
    high = value.astype(BF16)
    return high, (value - high.astype(F32)).astype(BF16)


def mm_split(left, right, dims=((1,), (0,))):
    return mm(left[0], right[0], dims) + (mm(left[0], right[1], dims) + mm(left[1], right[0], dims))


def blocks_of(width):
    count = width // LEAF
    return [(i, j) for i in range(count) for j in range(i, count)]


def gram_kernel(which_ref, x_ref, out_ref):
    pairs = blocks_of(x_ref.shape[1])
    half = len(pairs) // 2
    for part in range(2):

        @pl.when(which_ref[0] == part)
        def _():
            mine = pairs[part * half : (part + 1) * half]
            for i in sorted({pair[0] // 2 * 2 for pair in mine}):
                inside = [pair for pair in mine if pair[0] in (i, i + 1)]
                top, bottom = inside[0][0], inside[-1][0] + 1
                left, right = min(j for _, j in inside), max(j for _, j in inside) + 1
                rows, columns = slice(top * LEAF, bottom * LEAF), slice(left * LEAF, right * LEAF)
                product = mm(x_ref[:, rows], x_ref[:, columns], ((0,), (0,)))
                for row, j in inside:
                    at = mine.index((row, j)) * LEAF
                    down, over = (row - top) * LEAF, (j - left) * LEAF
                    out_ref[at : at + LEAF, :] = product[down : down + LEAF, over : over + LEAF]


def gram_half(features, which):
    rows = len(blocks_of(features.shape[1])) // 2 * LEAF
    return pl.pallas_call(
        gram_kernel,
        out_shape=jax.ShapeDtypeStruct((rows, LEAF), F32),
        in_specs=[SMEM, VMEM],
        out_specs=VMEM,
        compiler_params=ROOM,
        name="gram_half",
    )(which, features)


def cut_along(sources, first, rows, axis, at):
    count = GRID[axis]
    rows = rows // count

    def piece(d):
        start = first + (at + d) % count * rows
        return sum(lax.dynamic_slice_in_dim(source, start, rows, 0) for source in sources)

    return [shifted(piece(d), axis, d) for d in range(1, count)] + [piece(0)]


def gathered_along(piece, axis):
    return [piece] + [shifted(piece, axis, d) for d in range(1, GRID[axis])]


def onward(pieces):
    return jnp.concatenate([pieces[0]] + pieces[:0:-1], axis=0)


def summed(kept, taken, core, at, target_features):
    rows = kept.shape[0] // 2
    orders = ((Y, X), (X, Y))
    first = [cut_along([kept, taken], n * rows, rows, order[0], at[order[0]]) for n, order in enumerate(orders)]
    second = []
    for order, sources in zip(orders, first):
        second.append(cut_along(sources, 0, rows // GRID[order[0]], order[1], at[order[1]]))
    share = jnp.concatenate([sum(sources) for sources in second], axis=0)
    share, late = lax.optimization_barrier((share, target_features))
    late = [passed_along(late, d) for d in range(2, STEPS)]
    for mask in (1, 3, 7):
        share = share + swapped(share, Z, mask)
    share, late = lax.optimization_barrier((share, late))
    least = share.shape[0] // 2
    pieces, numbers = [], []
    for n, order in enumerate(orders):
        near, far = order[1], order[0]
        part = onward(gathered_along(share[n * least : (n + 1) * least], near))
        for d, piece in enumerate(gathered_along(part, far)):
            pieces.append(piece)
            numbers += [
                (n * GRID[far] + (at[far] - d) % GRID[far]) * GRID[near] + (at[near] + r) % GRID[near]
                for r in range(GRID[near])
            ]
    numbers = jnp.stack(numbers).astype(jnp.int32)
    half = kept.shape[0] // least
    mine = jnp.concatenate(pieces, axis=0)
    pieces = [mine, swapped(mine, CORE, 1)]
    return pieces, jnp.concatenate([numbers + core * half, numbers + (1 - core) * half]), late


def invert(rows, meanwhile):
    rows = list(rows)
    count, shape = len(rows), rows[0].shape
    per_band = BAND // GROUP
    lane = lax.broadcasted_iota(jnp.int32, shape, 1)
    sub = lax.broadcasted_iota(jnp.int32, shape, 0)

    def column(value, at):
        return jnp.take_along_axis(value, jnp.full(shape, at, jnp.int32), axis=1)

    def row(value, at):
        return jnp.broadcast_to(value[at : at + 1, :], shape)

    for g in range(count):
        first = GROUP * g
        band = range(g // per_band * per_band, (g // per_band + 1) * per_band)
        inside = (lane >= first) & (lane < first + GROUP)
        columns = [column(rows[g], first + q) for q in range(GROUP)]
        wide = jnp.where(inside, jnp.where(lane - first == sub, 1.0, 0.0), rows[g])
        for p in range(0, GROUP, 2):
            u, v = columns[p], columns[p + 1]
            a, b, c, d = row(u, p), row(v, p), row(u, p + 1), row(v, p + 1)
            scale = 1.0 / (a * d - b * c)

            def eliminated(value):
                r0, r1 = row(value, p), row(value, p + 1)
                n0 = (d * r0 - b * r1) * scale
                n1 = (a * r1 - c * r0) * scale
                return jnp.where(sub == p, n0, jnp.where(sub == p + 1, n1, value - u * n0 - v * n1))

            for q in range(p + 2, GROUP):
                columns[q] = eliminated(columns[q])
            wide = eliminated(wide)
        pivot_rows = [row(wide, q) for q in range(GROUP)]
        for i in [band[(g + 1 + n) % per_band] for n in range(per_band - 1)]:
            terms = [column(rows[i], first + q) * pivot_rows[q] for q in range(GROUP)]
            while len(terms) > 1:
                terms = [terms[n] + terms[n + 1] for n in range(0, len(terms), 2)]
            rows[i] = jnp.where(inside, 0.0, rows[i]) - terms[0]
        rows[g] = wide
        meanwhile(g)
        if g == band[-1]:
            swept = (lane >= GROUP * band[0]) & (lane < GROUP * (band[-1] + 1))
            others = [i for i in range(count) if i not in band]
            parts = split_wide(jnp.concatenate([jnp.where(swept, rows[i], 0.0) for i in others], axis=0))
            high, middle, low = [(part.astype(F32), pltpu.roll(part.astype(F32), BAND, 1)) for part in parts]
            here, there = (0, 1) if band[0] == 0 else (1, 0)
            left = [high[here] + high[there], high[here] + middle[there], middle[here] + low[there]]
            above, between, below = split_wide(jnp.concatenate([rows[i] for i in band], axis=0))
            product = mm(
                jnp.concatenate(left, axis=1).astype(BF16),
                jnp.concatenate([above, between, below, above, between, above], axis=0),
            )
            for n, i in enumerate(others):
                rows[i] = jnp.where(swept, 0.0, rows[i]) - product[n * GROUP : (n + 1) * GROUP]
    return rows


def attribution_kernel(scale, pieces, where_ref, *refs):
    piece_refs, target_refs = refs[:pieces], refs[pieces : pieces + STEPS]
    x_hbm, out_hbm, packed_ref, m_ref, left_ref, right_ref, solved_ref, x_ref, t_ref, out_ref, sems = refs[
        pieces + STEPS :
    ]
    examples, width = x_ref.shape
    asked = out_ref.shape[1]
    per_block = asked // STEPS
    load_x = pltpu.make_async_copy(x_hbm, x_ref, sems.at[0])
    load_targets = [
        pltpu.make_async_copy(target, t_ref.at[pl.ds(j * per_block, per_block)], sems.at[1 + j])
        for j, target in enumerate(target_refs)
    ]
    for load in load_targets:
        load.start()
    load_x.start()
    steps = width // LEAF
    slots = LEAF // GROUP
    cuts = where_ref.shape[0] // pieces
    rows = piece_refs[0].shape[0] // cuts
    for n in range(pieces * cuts):
        piece, first = piece_refs[n // cuts], n % cuts * rows
        packed_ref[pl.ds(pl.multiple_of(where_ref[n] * rows, 8), rows), :] = piece[first : first + rows, :]
    tile = (LEAF, LEAF)
    diagonal = lax.broadcasted_iota(jnp.int32, tile, 0) == lax.broadcasted_iota(jnp.int32, tile, 1)
    blocks = {pair: slice(n * LEAF, (n + 1) * LEAF) for n, pair in enumerate(blocks_of(width))}
    total = jnp.zeros(tile, F32)
    for j in range(steps):
        total = total + jnp.where(diagonal, packed_ref[blocks[j, j], :], 0.0)
    damping = 0.1 * jnp.sum(total, keepdims=True) / width

    targets_at, examples_at, m_rows = width, width + asked, width + asked + examples

    def unpack(i, j):
        block = packed_ref[blocks[i, j], :]
        if i == j:
            m_ref[i * LEAF : (i + 1) * LEAF, j * LEAF : (j + 1) * LEAF] = block + jnp.where(diagonal, damping, 0.0)
        else:
            m_ref[i * LEAF : (i + 1) * LEAF, j * LEAF : (j + 1) * LEAF] = block
            m_ref[j * LEAF : (j + 1) * LEAF, i * LEAF : (i + 1) * LEAF] = block.T

    def widen(source, first, at, count):
        m_ref[at : at + count, :] = source[first : first + count, :].astype(F32)

    def both(ref, at, value, down):
        high, low = split(value)
        for n, part in enumerate((high, low, high) if down else (high, high, low)):
            if down:
                ref[n * LEAF : (n + 1) * LEAF, at : at + value.shape[1]] = part
            else:
                ref[at : at + value.shape[0], n * LEAF : (n + 1) * LEAF] = part

    def product_columns(inverse, lo, first, last):
        both(right_ref, first, mm_wide(inverse, m_ref[lo : lo + LEAF, first:last]), True)

    def split_rows(lo, first, last):
        both(left_ref, first, m_ref[first:last, lo : lo + LEAF], False)

    def update(r0, r1, c0, c1):
        m_ref[r0:r1, c0:c1] = m_ref[r0:r1, c0:c1] - mm(left_ref[r0:r1, :], right_ref[:, c0:c1])

    def weigh_targets(inverse, lo):
        high, low = split(mm_split(split(m_ref[targets_at:examples_at, lo : lo + LEAF]), split(inverse * scale)))
        for n, part in enumerate((high, low, high)):
            solved_ref[:, n * LEAF : (n + 1) * LEAF] = part

    def score(j, first, last):
        part = mm(left_ref[examples_at + first : examples_at + last, :], solved_ref[...], ((1,), (1,)))
        out_ref[first:last, :] = part if j == 0 else out_ref[first:last, :] + part

    def jobs_after(j, inverse):
        lo, hi = j * LEAF, (j + 1) * LEAF
        tall = [(r, min(r + 512, width)) for r in range(hi, width, 512)]
        tall += [(r, r + 512) for r in range(targets_at, m_rows, 512)]
        jobs = []
        if hi + LEAF < width:
            jobs.append(lambda: product_columns(inverse, lo, hi + LEAF, width))
        jobs.append(lambda: weigh_targets(inverse, lo))
        for r0, r1 in tall:
            fresh = max(r0, hi + LEAF) if r0 < targets_at else r0
            if fresh < r1:
                jobs.append(functools.partial(split_rows, lo, fresh, r1))
            if r0 >= targets_at:
                for c in range(hi, width, 256):
                    jobs.append(functools.partial(update, r0, r1, c, min(c + 256, width)))
                continue
            if fresh < r1:
                jobs.append(functools.partial(update, fresh, r1, hi, hi + LEAF))
            for c in range(hi + LEAF, width, 256):
                jobs.append(functools.partial(update, r0, r1, c, min(c + 256, width)))
        for r in range(0, examples, 256):
            jobs.append(functools.partial(score, j, r, r + 256))
        return jobs

    unpack(0, 0)
    jobs = [functools.partial(unpack, i, j) for i, j in blocks if (i, j) != (0, 0)]
    for j, load in enumerate(load_targets):
        jobs.append(load.wait)
        jobs.append(functools.partial(widen, t_ref, j * per_block, targets_at + j * per_block, per_block))
    jobs.append(load_x.wait)
    for r in range(0, examples, 256):
        jobs.append(functools.partial(widen, x_ref, r, examples_at + r, 256))
    for j in range(steps):
        lo, hi = j * LEAF, (j + 1) * LEAF

        def meanwhile(g):
            for job in jobs[g * len(jobs) // slots : (g + 1) * len(jobs) // slots]:
                job()

        groups = [m_ref[lo + GROUP * i : lo + GROUP * (i + 1), lo:hi] for i in range(slots)]
        inverse = jnp.concatenate(invert(groups, meanwhile), axis=0)
        if hi < width:
            product_columns(inverse, lo, hi, hi + LEAF)
            split_rows(lo, hi, hi + LEAF)
            update(hi, hi + LEAF, hi, hi + LEAF)
            jobs = jobs_after(j, inverse)
    weigh_targets(inverse, lo)
    split_rows(lo, examples_at, m_rows)
    stores = []
    for n, r in enumerate(range(0, examples, 256)):
        score(steps - 1, r, r + 256)
        stores.append(
            pltpu.make_async_copy(
                out_ref.at[pl.ds(r, 256)], out_hbm.at[pl.ds(r, 256)], sems.at[1 + STEPS + n]
            )
        )
        stores[-1].start()
    for store in stores:
        store.wait()


def attribute(pieces, where, targets, x, scale):
    width = x.shape[1]
    asked = STEPS * targets[0].shape[0]
    packed = sum(piece.shape[0] for piece in pieces)
    return pl.pallas_call(
        functools.partial(attribution_kernel, scale, len(pieces)),
        out_shape=jax.ShapeDtypeStruct((x.shape[0], asked), F32),
        in_specs=[SMEM] + [VMEM] * len(pieces) + [ANY] * (STEPS + 1),
        out_specs=ANY,
        scratch_shapes=[
            pltpu.VMEM((packed, LEAF), F32),
            pltpu.VMEM((width + asked + x.shape[0], width), F32),
            pltpu.VMEM((width + asked + x.shape[0], 3 * LEAF), BF16),
            pltpu.VMEM((3 * LEAF, width), BF16),
            pltpu.VMEM((asked, 3 * LEAF), BF16),
            pltpu.VMEM(x.shape, BF16),
            pltpu.VMEM((asked, width), BF16),
            pltpu.VMEM((x.shape[0], asked), F32),
            pltpu.SemaphoreType.DMA((1 + STEPS + x.shape[0] // 256,)),
        ],
        compiler_params=ROOM,
        name="attribute",
    )(where, *pieces, *targets, x)


def local(train_features, target_features):
    width = train_features.shape[1]
    examples = train_features.shape[0] * math.prod(GRID)
    device = lax.axis_index("dp")
    core = device % GRID[CORE]
    at = {X: device // GRID[CORE] % GRID[X], Y: device // math.prod(GRID[Z:])}
    early = passed_along(target_features, 1)
    sent = gram_half(train_features, (1 - core).reshape(1))
    taken = swapped(sent, CORE, 1)
    kept = gram_half(train_features, core.reshape(1))
    kept, taken, early = lax.optimization_barrier((kept, taken, early))
    pieces, where, late = summed(kept, taken, core, at, target_features)
    targets = [target_features, early] + late
    return attribute(pieces, where, targets, train_features, math.sqrt(examples / width))


def solution(mesh):
    placed = (P("dp", None), P("dp", None))
    return jax.shard_map(local, mesh=mesh, in_specs=placed, out_specs=P("dp", None), check_vma=False)
```

```python
import functools
import math

import jax
import jax.numpy as jnp
from jax import lax
from jax.experimental import pallas as pl
from jax.experimental.pallas import tpu as pltpu
from jax.sharding import PartitionSpec as P

STEPS = 4
LEAF = 128
GROUP = 8
BAND = 64
GRID = (4, 8, 4, 2)
Y, Z, X, CORE = range(4)
F32 = jnp.float32
BF16 = jnp.bfloat16
VMEM = pl.BlockSpec(memory_space=pltpu.VMEM)
ANY = pl.BlockSpec(memory_space=pl.ANY)
SMEM = pl.BlockSpec(memory_space=pltpu.SMEM)
ROOM = pltpu.CompilerParams(vmem_limit_bytes=56 * 1024 * 1024)


def place(device):
    where = []
    for size in reversed(GRID):
        where.append(device % size)
        device //= size
    return where[::-1]


def device_at(where):
    device = 0
    for size, at in zip(GRID, where):
        device = device * size + at
    return device


def along(axis, move):
    route = []
    for device in range(math.prod(GRID)):
        where = place(device)
        where[axis] = move(where[axis]) % GRID[axis]
        route.append((device, device_at(where)))
    return route


def shifted(block, axis, distance):
    return lax.ppermute(block, "dp", along(axis, lambda p: p + distance))


def swapped(block, axis, mask):
    return lax.ppermute(block, "dp", along(axis, lambda p: p ^ mask))


def passed_along(block, distance):
    devices = math.prod(GRID)
    return lax.ppermute(block, "dp", [((i - distance) % devices, i) for i in range(devices)])


def mm(left, right, dims=((1,), (0,))):
    return lax.dot_general(left, right, (dims, ((), ())), preferred_element_type=F32)


def split_wide(value):
    high = value.astype(BF16)
    rest = value - high.astype(F32)
    middle = rest.astype(BF16)
    return high, middle, (rest - middle.astype(F32)).astype(BF16)


def mm_wide(left, right):
    high, middle, low = split_wide(left)
    above, between, below = split_wide(right)
    return mm(
        jnp.concatenate([high, high, high, middle, middle, low], axis=1),
        jnp.concatenate([above, between, below, above, between, above], axis=0),
    )


def split(value):
    high = value.astype(BF16)
    return high, (value - high.astype(F32)).astype(BF16)


def mm_split(left, right, dims=((1,), (0,))):
    return mm(left[0], right[0], dims) + (mm(left[0], right[1], dims) + mm(left[1], right[0], dims))


def blocks_of(width):
    count = width // LEAF
    return [(i, j) for i in range(count) for j in range(i, count)]


def gram_kernel(which_ref, x_ref, out_ref):
    pairs = blocks_of(x_ref.shape[1])
    half = len(pairs) // 2
    for part in range(2):

        @pl.when(which_ref[0] == part)
        def _():
            mine = pairs[part * half : (part + 1) * half]
            for i in sorted({pair[0] // 2 * 2 for pair in mine}):
                inside = [pair for pair in mine if pair[0] in (i, i + 1)]
                top, bottom = inside[0][0], inside[-1][0] + 1
                left, right = min(j for _, j in inside), max(j for _, j in inside) + 1
                rows, columns = slice(top * LEAF, bottom * LEAF), slice(left * LEAF, right * LEAF)
                product = mm(x_ref[:, rows], x_ref[:, columns], ((0,), (0,)))
                for row, j in inside:
                    at = mine.index((row, j)) * LEAF
                    down, over = (row - top) * LEAF, (j - left) * LEAF
                    out_ref[at : at + LEAF, :] = product[down : down + LEAF, over : over + LEAF]


def gram_half(features, which):
    rows = len(blocks_of(features.shape[1])) // 2 * LEAF
    return pl.pallas_call(
        gram_kernel,
        out_shape=jax.ShapeDtypeStruct((rows, LEAF), F32),
        in_specs=[SMEM, VMEM],
        out_specs=VMEM,
        compiler_params=ROOM,
        name="gram_half",
    )(which, features)


def cut_along(sources, first, rows, axis, at):
    count = GRID[axis]
    rows = rows // count

    def piece(d):
        start = first + (at + d) % count * rows
        return sum(lax.dynamic_slice_in_dim(source, start, rows, 0) for source in sources)

    return [shifted(piece(d), axis, d) for d in range(1, count)] + [piece(0)]


RING = (0, 1, 3, 2)


def doubled(part, axis, mask):
    return jnp.concatenate([part, swapped(part, axis, mask)], axis=0)


def summed(kept, taken, core, at, target_features):
    rows = kept.shape[0] // 2
    orders = ((Y, X), (X, Y))
    first = [cut_along([kept, taken], n * rows, rows, order[0], at[order[0]]) for n, order in enumerate(orders)]
    second = []
    for order, sources in zip(orders, first):
        second.append(cut_along(sources, 0, rows // GRID[order[0]], order[1], at[order[1]]))
    share = jnp.concatenate([sum(sources) for sources in second], axis=0)
    share, late = lax.optimization_barrier((share, target_features))
    late = [passed_along(late, d) for d in range(2, STEPS)]
    for mask in (1, 3, 7):
        share = share + swapped(share, Z, mask)
    share, late = lax.optimization_barrier((share, late))
    least = share.shape[0] // 2
    parts = [share[:least], share[least:]]
    for mask in (RING[1], RING[2]):
        parts = [doubled(part, order[1], mask) for part, order in zip(parts, orders)]
    parts = [doubled(part, order[0], RING[1]) for part, order in zip(parts, orders)]
    parts += [swapped(part, order[0], RING[2]) for part, order in zip(parts, orders)]
    parts += [swapped(part, CORE, 1) for part in parts]
    half = kept.shape[0] // least
    numbers = []
    for side in (core * half, (1 - core) * half):
        for masks in (RING[:2], RING[2:]):
            for n, (far, near) in enumerate(orders):
                numbers += [
                    side + (n * GRID[far] + (at[far] ^ m)) * GRID[near] + (at[near] ^ r) for m in masks for r in RING
                ]
    return parts, jnp.stack(numbers).astype(jnp.int32), late


def invert(rows, meanwhile):
    rows = list(rows)
    count, shape = len(rows), rows[0].shape
    per_band = BAND // GROUP
    lane = lax.broadcasted_iota(jnp.int32, shape, 1)
    sub = lax.broadcasted_iota(jnp.int32, shape, 0)

    def column(value, at):
        return jnp.take_along_axis(value, jnp.full(shape, at, jnp.int32), axis=1)

    def row(value, at):
        return jnp.broadcast_to(value[at : at + 1, :], shape)

    for g in range(count):
        first = GROUP * g
        band = range(g // per_band * per_band, (g // per_band + 1) * per_band)
        inside = (lane >= first) & (lane < first + GROUP)
        columns = [column(rows[g], first + q) for q in range(GROUP)]
        wide = jnp.where(inside, jnp.where(lane - first == sub, 1.0, 0.0), rows[g])
        for p in range(0, GROUP, 2):
            u, v = columns[p], columns[p + 1]
            a, b, c, d = row(u, p), row(v, p), row(u, p + 1), row(v, p + 1)
            scale = 1.0 / (a * d - b * c)

            def eliminated(value):
                r0, r1 = row(value, p), row(value, p + 1)
                n0 = (d * r0 - b * r1) * scale
                n1 = (a * r1 - c * r0) * scale
                return jnp.where(sub == p, n0, jnp.where(sub == p + 1, n1, value - u * n0 - v * n1))

            for q in range(p + 2, GROUP):
                columns[q] = eliminated(columns[q])
            wide = eliminated(wide)
        pivot_rows = [row(wide, q) for q in range(GROUP)]
        for i in [band[(g + 1 + n) % per_band] for n in range(per_band - 1)]:
            terms = [column(rows[i], first + q) * pivot_rows[q] for q in range(GROUP)]
            while len(terms) > 1:
                terms = [terms[n] + terms[n + 1] for n in range(0, len(terms), 2)]
            rows[i] = jnp.where(inside, 0.0, rows[i]) - terms[0]
        rows[g] = wide
        meanwhile(g)
        if g == band[-1]:
            swept = (lane >= GROUP * band[0]) & (lane < GROUP * (band[-1] + 1))
            others = [i for i in range(count) if i not in band]
            parts = split_wide(jnp.concatenate([jnp.where(swept, rows[i], 0.0) for i in others], axis=0))
            high, middle, low = [(part.astype(F32), pltpu.roll(part.astype(F32), BAND, 1)) for part in parts]
            here, there = (0, 1) if band[0] == 0 else (1, 0)
            left = [high[here] + high[there], high[here] + middle[there], middle[here] + low[there]]
            above, between, below = split_wide(jnp.concatenate([rows[i] for i in band], axis=0))
            product = mm(
                jnp.concatenate(left, axis=1).astype(BF16),
                jnp.concatenate([above, between, below, above, between, above], axis=0),
            )
            for n, i in enumerate(others):
                rows[i] = jnp.where(swept, 0.0, rows[i]) - product[n * GROUP : (n + 1) * GROUP]
    return rows


def attribution_kernel(scale, pieces, where_ref, *refs):
    piece_refs, target_refs = refs[:pieces], refs[pieces : pieces + STEPS]
    x_hbm, out_hbm, packed_ref, m_ref, left_ref, right_ref, solved_ref, x_ref, t_ref, out_ref, sems = refs[
        pieces + STEPS :
    ]
    examples, width = x_ref.shape
    asked = out_ref.shape[1]
    per_block = asked // STEPS
    load_x = pltpu.make_async_copy(x_hbm, x_ref, sems.at[0])
    load_targets = [
        pltpu.make_async_copy(target, t_ref.at[pl.ds(j * per_block, per_block)], sems.at[1 + j])
        for j, target in enumerate(target_refs)
    ]
    for load in load_targets:
        load.start()
    load_x.start()
    steps = width // LEAF
    slots = LEAF // GROUP
    cuts = where_ref.shape[0] // pieces
    rows = piece_refs[0].shape[0] // cuts
    for n in range(pieces * cuts):
        piece, first = piece_refs[n // cuts], n % cuts * rows
        packed_ref[pl.ds(pl.multiple_of(where_ref[n] * rows, 8), rows), :] = piece[first : first + rows, :]
    tile = (LEAF, LEAF)
    diagonal = lax.broadcasted_iota(jnp.int32, tile, 0) == lax.broadcasted_iota(jnp.int32, tile, 1)
    blocks = {pair: slice(n * LEAF, (n + 1) * LEAF) for n, pair in enumerate(blocks_of(width))}
    total = jnp.zeros(tile, F32)
    for j in range(steps):
        total = total + jnp.where(diagonal, packed_ref[blocks[j, j], :], 0.0)
    damping = 0.1 * jnp.sum(total, keepdims=True) / width

    targets_at, examples_at, m_rows = width, width + asked, width + asked + examples

    def unpack(i, j):
        block = packed_ref[blocks[i, j], :]
        if i == j:
            m_ref[i * LEAF : (i + 1) * LEAF, j * LEAF : (j + 1) * LEAF] = block + jnp.where(diagonal, damping, 0.0)
        else:
            m_ref[i * LEAF : (i + 1) * LEAF, j * LEAF : (j + 1) * LEAF] = block
            m_ref[j * LEAF : (j + 1) * LEAF, i * LEAF : (i + 1) * LEAF] = block.T

    def widen(source, first, at, count):
        m_ref[at : at + count, :] = source[first : first + count, :].astype(F32)

    def both(ref, at, value, down):
        high, low = split(value)
        for n, part in enumerate((high, low, high) if down else (high, high, low)):
            if down:
                ref[n * LEAF : (n + 1) * LEAF, at : at + value.shape[1]] = part
            else:
                ref[at : at + value.shape[0], n * LEAF : (n + 1) * LEAF] = part

    def product_columns(inverse, lo, first, last):
        both(right_ref, first, mm_wide(inverse, m_ref[lo : lo + LEAF, first:last]), True)

    def split_rows(lo, first, last):
        both(left_ref, first, m_ref[first:last, lo : lo + LEAF], False)

    def update(r0, r1, c0, c1):
        m_ref[r0:r1, c0:c1] = m_ref[r0:r1, c0:c1] - mm(left_ref[r0:r1, :], right_ref[:, c0:c1])

    def weigh_targets(inverse, lo):
        high, low = split(mm_split(split(m_ref[targets_at:examples_at, lo : lo + LEAF]), split(inverse * scale)))
        for n, part in enumerate((high, low, high)):
            solved_ref[:, n * LEAF : (n + 1) * LEAF] = part

    def score(j, first, last):
        part = mm(left_ref[examples_at + first : examples_at + last, :], solved_ref[...], ((1,), (1,)))
        out_ref[first:last, :] = part if j == 0 else out_ref[first:last, :] + part

    def jobs_after(j, inverse):
        lo, hi = j * LEAF, (j + 1) * LEAF
        tall = [(r, min(r + 512, width)) for r in range(hi, width, 512)]
        tall += [(r, r + 512) for r in range(targets_at, m_rows, 512)]
        jobs = []
        if hi + LEAF < width:
            jobs.append(lambda: product_columns(inverse, lo, hi + LEAF, width))
        jobs.append(lambda: weigh_targets(inverse, lo))
        for r0, r1 in tall:
            fresh = max(r0, hi + LEAF) if r0 < targets_at else r0
            if fresh < r1:
                jobs.append(functools.partial(split_rows, lo, fresh, r1))
            if r0 >= targets_at:
                for c in range(hi, width, 256):
                    jobs.append(functools.partial(update, r0, r1, c, min(c + 256, width)))
                continue
            if fresh < r1:
                jobs.append(functools.partial(update, fresh, r1, hi, hi + LEAF))
            for c in range(hi + LEAF, width, 256):
                jobs.append(functools.partial(update, r0, r1, c, min(c + 256, width)))
        for r in range(0, examples, 256):
            jobs.append(functools.partial(score, j, r, r + 256))
        return jobs

    unpack(0, 0)
    jobs = [functools.partial(unpack, i, j) for i, j in blocks if (i, j) != (0, 0)]
    for j, load in enumerate(load_targets):
        jobs.append(load.wait)
        jobs.append(functools.partial(widen, t_ref, j * per_block, targets_at + j * per_block, per_block))
    jobs.append(load_x.wait)
    for r in range(0, examples, 256):
        jobs.append(functools.partial(widen, x_ref, r, examples_at + r, 256))
    for j in range(steps):
        lo, hi = j * LEAF, (j + 1) * LEAF

        def meanwhile(g):
            for job in jobs[g * len(jobs) // slots : (g + 1) * len(jobs) // slots]:
                job()

        groups = [m_ref[lo + GROUP * i : lo + GROUP * (i + 1), lo:hi] for i in range(slots)]
        inverse = jnp.concatenate(invert(groups, meanwhile), axis=0)
        if hi < width:
            product_columns(inverse, lo, hi, hi + LEAF)
            split_rows(lo, hi, hi + LEAF)
            update(hi, hi + LEAF, hi, hi + LEAF)
            jobs = jobs_after(j, inverse)
    weigh_targets(inverse, lo)
    split_rows(lo, examples_at, m_rows)
    stores = []
    for n, r in enumerate(range(0, examples, 256)):
        score(steps - 1, r, r + 256)
        stores.append(
            pltpu.make_async_copy(
                out_ref.at[pl.ds(r, 256)], out_hbm.at[pl.ds(r, 256)], sems.at[1 + STEPS + n]
            )
        )
        stores[-1].start()
    for store in stores:
        store.wait()


def attribute(pieces, where, targets, x, scale):
    width = x.shape[1]
    asked = STEPS * targets[0].shape[0]
    packed = sum(piece.shape[0] for piece in pieces)
    return pl.pallas_call(
        functools.partial(attribution_kernel, scale, len(pieces)),
        out_shape=jax.ShapeDtypeStruct((x.shape[0], asked), F32),
        in_specs=[SMEM] + [VMEM] * len(pieces) + [ANY] * (STEPS + 1),
        out_specs=ANY,
        scratch_shapes=[
            pltpu.VMEM((packed, LEAF), F32),
            pltpu.VMEM((width + asked + x.shape[0], width), F32),
            pltpu.VMEM((width + asked + x.shape[0], 3 * LEAF), BF16),
            pltpu.VMEM((3 * LEAF, width), BF16),
            pltpu.VMEM((asked, 3 * LEAF), BF16),
            pltpu.VMEM(x.shape, BF16),
            pltpu.VMEM((asked, width), BF16),
            pltpu.VMEM((x.shape[0], asked), F32),
            pltpu.SemaphoreType.DMA((1 + STEPS + x.shape[0] // 256,)),
        ],
        compiler_params=ROOM,
        name="attribute",
    )(where, *pieces, *targets, x)


def local(train_features, target_features):
    width = train_features.shape[1]
    examples = train_features.shape[0] * math.prod(GRID)
    device = lax.axis_index("dp")
    core = device % GRID[CORE]
    at = {X: device // GRID[CORE] % GRID[X], Y: device // math.prod(GRID[Z:])}
    early = passed_along(target_features, 1)
    sent = gram_half(train_features, (1 - core).reshape(1))
    taken = swapped(sent, CORE, 1)
    kept = gram_half(train_features, core.reshape(1))
    kept, taken, early = lax.optimization_barrier((kept, taken, early))
    pieces, where, late = summed(kept, taken, core, at, target_features)
    targets = [target_features, early] + late
    return attribute(pieces, where, targets, train_features, math.sqrt(examples / width))


def solution(mesh):
    placed = (P("dp", None), P("dp", None))
    return jax.shard_map(local, mesh=mesh, in_specs=placed, out_specs=P("dp", None), check_vma=False)
```

```python
import functools
import math

import jax
import jax.numpy as jnp
from jax import lax
from jax.experimental import pallas as pl
from jax.experimental.pallas import tpu as pltpu
from jax.sharding import PartitionSpec as P

STEPS = 4
LEAF = 128
GROUP = 8
BAND = 64
GRID = (4, 8, 4, 2)
Y, Z, X, CORE = range(4)
F32 = jnp.float32
BF16 = jnp.bfloat16
VMEM = pl.BlockSpec(memory_space=pltpu.VMEM)
ANY = pl.BlockSpec(memory_space=pl.ANY)
SMEM = pl.BlockSpec(memory_space=pltpu.SMEM)
ROOM = pltpu.CompilerParams(vmem_limit_bytes=56 * 1024 * 1024)


def place(device):
    where = []
    for size in reversed(GRID):
        where.append(device % size)
        device //= size
    return where[::-1]


def device_at(where):
    device = 0
    for size, at in zip(GRID, where):
        device = device * size + at
    return device


def along(axis, move):
    route = []
    for device in range(math.prod(GRID)):
        where = place(device)
        where[axis] = move(where[axis]) % GRID[axis]
        route.append((device, device_at(where)))
    return route


def shifted(block, axis, distance):
    return lax.ppermute(block, "dp", along(axis, lambda p: p + distance))


def swapped(block, axis, mask):
    return lax.ppermute(block, "dp", along(axis, lambda p: p ^ mask))


def passed_along(block, distance):
    devices = math.prod(GRID)
    return lax.ppermute(block, "dp", [((i - distance) % devices, i) for i in range(devices)])


def mm(left, right, dims=((1,), (0,))):
    return lax.dot_general(left, right, (dims, ((), ())), preferred_element_type=F32)


def split_wide(value):
    high = value.astype(BF16)
    rest = value - high.astype(F32)
    middle = rest.astype(BF16)
    return high, middle, (rest - middle.astype(F32)).astype(BF16)


def mm_wide(left, right):
    high, middle, low = split_wide(left)
    above, between, below = split_wide(right)
    return mm(
        jnp.concatenate([high, high, high, middle, middle, low], axis=1),
        jnp.concatenate([above, between, below, above, between, above], axis=0),
    )


def split(value):
    high = value.astype(BF16)
    return high, (value - high.astype(F32)).astype(BF16)


def mm_split(left, right, dims=((1,), (0,))):
    return mm(left[0], right[0], dims) + (mm(left[0], right[1], dims) + mm(left[1], right[0], dims))


def blocks_of(width):
    count = width // LEAF
    return [(i, j) for i in range(count) for j in range(i, count)]


def gram_kernel(which_ref, x_ref, out_ref):
    pairs = blocks_of(x_ref.shape[1])
    half = len(pairs) // 2
    for part in range(2):

        @pl.when(which_ref[0] == part)
        def _():
            mine = pairs[part * half : (part + 1) * half]
            for i in sorted({pair[0] // 2 * 2 for pair in mine}):
                inside = [pair for pair in mine if pair[0] in (i, i + 1)]
                top, bottom = inside[0][0], inside[-1][0] + 1
                left, right = min(j for _, j in inside), max(j for _, j in inside) + 1
                rows, columns = slice(top * LEAF, bottom * LEAF), slice(left * LEAF, right * LEAF)
                product = mm(x_ref[:, rows], x_ref[:, columns], ((0,), (0,)))
                for row, j in inside:
                    at = mine.index((row, j)) * LEAF
                    down, over = (row - top) * LEAF, (j - left) * LEAF
                    out_ref[at : at + LEAF, :] = product[down : down + LEAF, over : over + LEAF]


def gram_half(features, which):
    rows = len(blocks_of(features.shape[1])) // 2 * LEAF
    return pl.pallas_call(
        gram_kernel,
        out_shape=jax.ShapeDtypeStruct((rows, LEAF), F32),
        in_specs=[SMEM, VMEM],
        out_specs=VMEM,
        compiler_params=ROOM,
        name="gram_half",
    )(which, features)


def halved(sources, first, rows, axis, mask, side):
    rows = rows // 2

    def part(which):
        return sum(lax.dynamic_slice_in_dim(source, first + which * rows, rows, 0) for source in sources)

    return [part(side), swapped(part(1 - side), axis, mask)]


RING = (0, 1, 3, 2)


def doubled(part, axis, mask):
    return jnp.concatenate([part, swapped(part, axis, mask)], axis=0)


def summed(kept, taken, core, at, target_features):
    rows = kept.shape[0] // 2
    orders = ((Y, X), (X, Y))
    held = [([kept, taken], n * rows) for n in range(len(orders))]
    for step, mask in ((0, 3), (0, 1), (1, 3), (1, 1)):
        sides = [at[order[step]] // 2 if mask == 3 else at[order[step]] % 2 for order in orders]
        held = [
            (halved(sources, first, rows, order[step], mask, side), 0)
            for (sources, first), order, side in zip(held, orders, sides)
        ]
        rows = rows // 2
    share = jnp.concatenate([sum(sources) for sources, _ in held], axis=0)
    share, late = lax.optimization_barrier((share, target_features))
    late = [passed_along(late, d) for d in range(2, STEPS)]
    for mask in (1, 3, 7):
        share = share + swapped(share, Z, mask)
    share, late = lax.optimization_barrier((share, late))
    least = share.shape[0] // 2
    parts = [share[:least], share[least:]]
    for mask in (RING[1], RING[2]):
        parts = [doubled(part, order[1], mask) for part, order in zip(parts, orders)]
    parts = [doubled(part, order[0], RING[1]) for part, order in zip(parts, orders)]
    parts += [swapped(part, order[0], RING[2]) for part, order in zip(parts, orders)]
    parts += [swapped(part, CORE, 1) for part in parts]
    half = kept.shape[0] // least
    numbers = []
    for side in (core * half, (1 - core) * half):
        for masks in (RING[:2], RING[2:]):
            for n, (far, near) in enumerate(orders):
                numbers += [
                    side + (n * GRID[far] + (at[far] ^ m)) * GRID[near] + (at[near] ^ r) for m in masks for r in RING
                ]
    return parts, jnp.stack(numbers).astype(jnp.int32), late


def invert(rows, meanwhile):
    rows = list(rows)
    count, shape = len(rows), rows[0].shape
    per_band = BAND // GROUP
    lane = lax.broadcasted_iota(jnp.int32, shape, 1)
    sub = lax.broadcasted_iota(jnp.int32, shape, 0)

    def column(value, at):
        return jnp.take_along_axis(value, jnp.full(shape, at, jnp.int32), axis=1)

    def row(value, at):
        return jnp.broadcast_to(value[at : at + 1, :], shape)

    for g in range(count):
        first = GROUP * g
        band = range(g // per_band * per_band, (g // per_band + 1) * per_band)
        inside = (lane >= first) & (lane < first + GROUP)
        columns = [column(rows[g], first + q) for q in range(GROUP)]
        wide = jnp.where(inside, jnp.where(lane - first == sub, 1.0, 0.0), rows[g])
        for p in range(0, GROUP, 2):
            u, v = columns[p], columns[p + 1]
            a, b, c, d = row(u, p), row(v, p), row(u, p + 1), row(v, p + 1)
            scale = 1.0 / (a * d - b * c)

            def eliminated(value):
                r0, r1 = row(value, p), row(value, p + 1)
                n0 = (d * r0 - b * r1) * scale
                n1 = (a * r1 - c * r0) * scale
                return jnp.where(sub == p, n0, jnp.where(sub == p + 1, n1, value - u * n0 - v * n1))

            for q in range(p + 2, GROUP):
                columns[q] = eliminated(columns[q])
            wide = eliminated(wide)
        pivot_rows = [row(wide, q) for q in range(GROUP)]
        for i in [band[(g + 1 + n) % per_band] for n in range(per_band - 1)]:
            terms = [column(rows[i], first + q) * pivot_rows[q] for q in range(GROUP)]
            while len(terms) > 1:
                terms = [terms[n] + terms[n + 1] for n in range(0, len(terms), 2)]
            rows[i] = jnp.where(inside, 0.0, rows[i]) - terms[0]
        rows[g] = wide
        meanwhile(g)
        if g == band[-1]:
            swept = (lane >= GROUP * band[0]) & (lane < GROUP * (band[-1] + 1))
            others = [i for i in range(count) if i not in band]
            parts = split_wide(jnp.concatenate([jnp.where(swept, rows[i], 0.0) for i in others], axis=0))
            high, middle, low = [(part.astype(F32), pltpu.roll(part.astype(F32), BAND, 1)) for part in parts]
            here, there = (0, 1) if band[0] == 0 else (1, 0)
            left = [high[here] + high[there], high[here] + middle[there], middle[here] + low[there]]
            above, between, below = split_wide(jnp.concatenate([rows[i] for i in band], axis=0))
            product = mm(
                jnp.concatenate(left, axis=1).astype(BF16),
                jnp.concatenate([above, between, below, above, between, above], axis=0),
            )
            for n, i in enumerate(others):
                rows[i] = jnp.where(swept, 0.0, rows[i]) - product[n * GROUP : (n + 1) * GROUP]
    return rows


def attribution_kernel(scale, pieces, where_ref, *refs):
    piece_refs, target_refs = refs[:pieces], refs[pieces : pieces + STEPS]
    x_hbm, out_hbm, packed_ref, m_ref, left_ref, right_ref, solved_ref, x_ref, t_ref, out_ref, sems = refs[
        pieces + STEPS :
    ]
    examples, width = x_ref.shape
    asked = out_ref.shape[1]
    per_block = asked // STEPS
    load_x = pltpu.make_async_copy(x_hbm, x_ref, sems.at[0])
    load_targets = [
        pltpu.make_async_copy(target, t_ref.at[pl.ds(j * per_block, per_block)], sems.at[1 + j])
        for j, target in enumerate(target_refs)
    ]
    for load in load_targets:
        load.start()
    load_x.start()
    steps = width // LEAF
    slots = LEAF // GROUP
    cuts = where_ref.shape[0] // pieces
    rows = piece_refs[0].shape[0] // cuts
    for n in range(pieces * cuts):
        piece, first = piece_refs[n // cuts], n % cuts * rows
        packed_ref[pl.ds(pl.multiple_of(where_ref[n] * rows, 8), rows), :] = piece[first : first + rows, :]
    tile = (LEAF, LEAF)
    diagonal = lax.broadcasted_iota(jnp.int32, tile, 0) == lax.broadcasted_iota(jnp.int32, tile, 1)
    blocks = {pair: slice(n * LEAF, (n + 1) * LEAF) for n, pair in enumerate(blocks_of(width))}
    total = jnp.zeros(tile, F32)
    for j in range(steps):
        total = total + jnp.where(diagonal, packed_ref[blocks[j, j], :], 0.0)
    damping = 0.1 * jnp.sum(total, keepdims=True) / width

    targets_at, examples_at, m_rows = width, width + asked, width + asked + examples

    def unpack(i, j):
        block = packed_ref[blocks[i, j], :]
        if i == j:
            m_ref[i * LEAF : (i + 1) * LEAF, j * LEAF : (j + 1) * LEAF] = block + jnp.where(diagonal, damping, 0.0)
        else:
            m_ref[i * LEAF : (i + 1) * LEAF, j * LEAF : (j + 1) * LEAF] = block
            m_ref[j * LEAF : (j + 1) * LEAF, i * LEAF : (i + 1) * LEAF] = block.T

    def widen(source, first, at, count):
        m_ref[at : at + count, :] = source[first : first + count, :].astype(F32)

    def both(ref, at, value, down):
        high, low = split(value)
        for n, part in enumerate((high, low, high) if down else (high, high, low)):
            if down:
                ref[n * LEAF : (n + 1) * LEAF, at : at + value.shape[1]] = part
            else:
                ref[at : at + value.shape[0], n * LEAF : (n + 1) * LEAF] = part

    def product_columns(inverse, lo, first, last):
        both(right_ref, first, mm_wide(inverse, m_ref[lo : lo + LEAF, first:last]), True)

    def split_rows(lo, first, last):
        both(left_ref, first, m_ref[first:last, lo : lo + LEAF], False)

    def update(r0, r1, c0, c1):
        m_ref[r0:r1, c0:c1] = m_ref[r0:r1, c0:c1] - mm(left_ref[r0:r1, :], right_ref[:, c0:c1])

    def weigh_targets(inverse, lo):
        high, low = split(mm_split(split(m_ref[targets_at:examples_at, lo : lo + LEAF]), split(inverse * scale)))
        for n, part in enumerate((high, low, high)):
            solved_ref[:, n * LEAF : (n + 1) * LEAF] = part

    def score(j, first, last):
        part = mm(left_ref[examples_at + first : examples_at + last, :], solved_ref[...], ((1,), (1,)))
        out_ref[first:last, :] = part if j == 0 else out_ref[first:last, :] + part

    def jobs_after(j, inverse):
        lo, hi = j * LEAF, (j + 1) * LEAF
        tall = [(r, min(r + 512, width)) for r in range(hi, width, 512)]
        tall += [(r, r + 512) for r in range(targets_at, m_rows, 512)]
        jobs = []
        if hi + LEAF < width:
            jobs.append(lambda: product_columns(inverse, lo, hi + LEAF, width))
        jobs.append(lambda: weigh_targets(inverse, lo))
        for r0, r1 in tall:
            fresh = max(r0, hi + LEAF) if r0 < targets_at else r0
            if fresh < r1:
                jobs.append(functools.partial(split_rows, lo, fresh, r1))
            if r0 >= targets_at:
                for c in range(hi, width, 256):
                    jobs.append(functools.partial(update, r0, r1, c, min(c + 256, width)))
                continue
            if fresh < r1:
                jobs.append(functools.partial(update, fresh, r1, hi, hi + LEAF))
            for c in range(hi + LEAF, width, 256):
                jobs.append(functools.partial(update, r0, r1, c, min(c + 256, width)))
        for r in range(0, examples, 256):
            jobs.append(functools.partial(score, j, r, r + 256))
        return jobs

    unpack(0, 0)
    jobs = [functools.partial(unpack, i, j) for i, j in blocks if (i, j) != (0, 0)]
    for j, load in enumerate(load_targets):
        jobs.append(load.wait)
        jobs.append(functools.partial(widen, t_ref, j * per_block, targets_at + j * per_block, per_block))
    jobs.append(load_x.wait)
    for r in range(0, examples, 256):
        jobs.append(functools.partial(widen, x_ref, r, examples_at + r, 256))
    for j in range(steps):
        lo, hi = j * LEAF, (j + 1) * LEAF

        def meanwhile(g):
            for job in jobs[g * len(jobs) // slots : (g + 1) * len(jobs) // slots]:
                job()

        groups = [m_ref[lo + GROUP * i : lo + GROUP * (i + 1), lo:hi] for i in range(slots)]
        inverse = jnp.concatenate(invert(groups, meanwhile), axis=0)
        if hi < width:
            product_columns(inverse, lo, hi, hi + LEAF)
            split_rows(lo, hi, hi + LEAF)
            update(hi, hi + LEAF, hi, hi + LEAF)
            jobs = jobs_after(j, inverse)
    weigh_targets(inverse, lo)
    split_rows(lo, examples_at, m_rows)
    stores = []
    for n, r in enumerate(range(0, examples, 256)):
        score(steps - 1, r, r + 256)
        stores.append(
            pltpu.make_async_copy(
                out_ref.at[pl.ds(r, 256)], out_hbm.at[pl.ds(r, 256)], sems.at[1 + STEPS + n]
            )
        )
        stores[-1].start()
    for store in stores:
        store.wait()


def attribute(pieces, where, targets, x, scale):
    width = x.shape[1]
    asked = STEPS * targets[0].shape[0]
    packed = sum(piece.shape[0] for piece in pieces)
    return pl.pallas_call(
        functools.partial(attribution_kernel, scale, len(pieces)),
        out_shape=jax.ShapeDtypeStruct((x.shape[0], asked), F32),
        in_specs=[SMEM] + [VMEM] * len(pieces) + [ANY] * (STEPS + 1),
        out_specs=ANY,
        scratch_shapes=[
            pltpu.VMEM((packed, LEAF), F32),
            pltpu.VMEM((width + asked + x.shape[0], width), F32),
            pltpu.VMEM((width + asked + x.shape[0], 3 * LEAF), BF16),
            pltpu.VMEM((3 * LEAF, width), BF16),
            pltpu.VMEM((asked, 3 * LEAF), BF16),
            pltpu.VMEM(x.shape, BF16),
            pltpu.VMEM((asked, width), BF16),
            pltpu.VMEM((x.shape[0], asked), F32),
            pltpu.SemaphoreType.DMA((1 + STEPS + x.shape[0] // 256,)),
        ],
        compiler_params=ROOM,
        name="attribute",
    )(where, *pieces, *targets, x)


def local(train_features, target_features):
    width = train_features.shape[1]
    examples = train_features.shape[0] * math.prod(GRID)
    device = lax.axis_index("dp")
    core = device % GRID[CORE]
    at = {X: device // GRID[CORE] % GRID[X], Y: device // math.prod(GRID[Z:])}
    early = passed_along(target_features, 1)
    sent = gram_half(train_features, (1 - core).reshape(1))
    taken = swapped(sent, CORE, 1)
    kept = gram_half(train_features, core.reshape(1))
    kept, taken, early = lax.optimization_barrier((kept, taken, early))
    pieces, where, late = summed(kept, taken, core, at, target_features)
    targets = [target_features, early] + late
    return attribute(pieces, where, targets, train_features, math.sqrt(examples / width))


def solution(mesh):
    placed = (P("dp", None), P("dp", None))
    return jax.shard_map(local, mesh=mesh, in_specs=placed, out_specs=P("dp", None), check_vma=False)
```
